256 devices in a mesh: dp: 8 (over y_hi, x), tensor: 32 (over y_lo, z, core).
Axes of the slice: x: 4, y: 4 (y_hi: 2, y_lo: 2; y = y_hi * 2 + y_lo), z: 8, core: 2. Of those that a mesh axis runs over, the one named last changes fastest.
Arguments:
- tokens: bfloat16 [512, 9216], P('tensor', 'dp'), may hold values from -6 to 6
- w_in: bfloat16 [9216, 36864], P('dp', 'tensor'), may hold values from -0.0625 to 0.0625
- w_out: bfloat16 [36864, 9216], P('tensor', 'dp'), may hold values from -0.03125 to 0.03125
- cotangent: bfloat16 [512, 9216], P('tensor', 'dp'), may hold values from -6 to 6
Outputs:
- output: bfloat16 [512, 9216], P('tensor', 'dp')
- input_grad: bfloat16 [512, 9216], P('tensor', 'dp')
- w_in_grad: bfloat16 [9216, 36864], P('dp', 'tensor')
- w_out_grad: bfloat16 [36864, 9216], P('tensor', 'dp')
The draws below stay inside these ranges and needn't reach their ends.
All inputs are finite; a program needn't handle non-finite values.
Results may differ from the reference program's by a relative error of at most 0.005.
Values may be sent and summed in bfloat16 or wider, within the bound.
A program may use at most 64 MiB of HBM per device.

```python
import math
import jax
import jax.numpy as jnp
from jax import lax

D = 9216
FF = 36864
TOKENS = 512


def level_of(rng, dims, pieces, least, largest):
    def one(axis_at, blocks):
        steps = jax.random.uniform(jax.random.fold_in(jax.random.fold_in(rng, 6), axis_at), (blocks,), jnp.float32, least / len(pieces), largest / len(pieces))
        return jnp.repeat(jnp.exp(steps), dims[axis_at] // blocks).reshape((-1,) + (1,) * (len(dims) - axis_at - 1))

    gain = one(*pieces[0])
    for cut in pieces[1:]:
        gain = gain * one(*cut)
    return gain


def scatter_about(rng, shape, deviation, reach, cuts=(), held_as=jnp.bfloat16):
    result = jax.random.normal(rng, shape, jnp.float32) * deviation
    if len(cuts) > 0:
        result = level_of(rng, shape, cuts, -0.22, 0.18) * result
    return jnp.clip(result, min=-reach, max=reach).astype(held_as)


def setup_inputs(seed: int = 0) -> dict:
    key_of = jax.random.split(jax.random.key(seed), 5)
    return {
        "tokens": scatter_about(key_of[0], (TOKENS, D), 1.0, 6.0, ((0, 32), (1, 8))),
        "w_in": scatter_about(key_of[1], (D, FF), D ** -0.5, 0.0625, ((0, 8), (1, 32))),
        "w_out": scatter_about(key_of[2], (FF, D), FF ** -0.5, 0.03125, ((0, 32), (1, 8))),
        "cotangent": scatter_about(key_of[3], (TOKENS, D), 1.0, 6.0, ((0, 32), (1, 8))),
    }


def gelu_value(v):
    return v * 0.5 * (1.0 + jax.scipy.special.erf(v / math.sqrt(2.0)))

def gelu_slope(v):
    cdf = 0.5 * (1.0 + jax.scipy.special.erf(v / math.sqrt(2.0)))
    return cdf + v * jnp.exp(-0.5 * v * v) / math.sqrt(2.0 * math.pi)

def reference(tokens, w_in, w_out, cotangent):
    hidden = jnp.dot(tokens, w_in, preferred_element_type=jnp.float32)
    activ = gelu_value(hidden).astype(jnp.bfloat16)
    output = jnp.dot(activ, w_out, preferred_element_type=jnp.float32).astype(jnp.bfloat16)
    grad_activ = lax.dot_general(cotangent, w_out, (((1,), (1,)), ((), ())), preferred_element_type=jnp.float32)
    grad_hidden = (grad_activ * gelu_slope(hidden)).astype(jnp.bfloat16)
    input_grad = lax.dot_general(grad_hidden, w_in, (((1,), (1,)), ((), ())), preferred_element_type=jnp.float32).astype(jnp.bfloat16)
    w_in_grad = lax.dot_general(tokens, grad_hidden, (((0,), (0,)), ((), ())), preferred_element_type=jnp.float32).astype(jnp.bfloat16)
    w_out_grad = lax.dot_general(activ, cotangent, (((0,), (0,)), ((), ())), preferred_element_type=jnp.float32).astype(jnp.bfloat16)
    return (output, input_grad, w_in_grad, w_out_grad)
```

```python
import functools
import math

import jax
import jax.numpy as jnp
from jax import lax
from jax.experimental import pallas as pl
from jax.experimental.pallas import tpu as pltpu
from jax.sharding import PartitionSpec as P

MESH = pl.DeviceIdType.MESH
ROWS = 512
W = 1152
OWN = 16
NX, NYH, NYL, NZ, NC = 4, 2, 2, 8, 2
NB = 4
RB = ROWS // NB
KO = NZ // NB
XR = RB // NX
YR = XR // NYH
OFFSETS = [[0, 1], [7, 2], [6, 3], [5, 4]]
TN = 384
N_MSG = 256


def gelu_value(v):
    return v * 0.5 * (1.0 + lax.erf(v * (1.0 / math.sqrt(2.0))))


def gelu_slope(v):
    cdf = 0.5 * (1.0 + lax.erf(v * (1.0 / math.sqrt(2.0))))
    return cdf + v * jnp.exp(-0.5 * v * v) * (1.0 / math.sqrt(2.0 * math.pi))


def block_kernel(
    tok_hbm, win_hbm, wout_hbm, cot_hbm,
    out_ref, ing_ref, t_out, c_out, a_out, g_out,
    win, wout, acts, part, sendp, xrecv, ysend, yrecv, ownp, slopes, mids,
    core_send, core_recv, tens_part, ylo_send, ylo_recv, fin_own, zsend, zrecv,
    local_sem, send_sem, recv_sem,
):
    d, t = lax.axis_index("dp"), lax.axis_index("tensor")
    yh, x = d // NX, d % NX
    yl, z, c = t // (NZ * NC), (t // NC) % NZ, t % NC

    def at_x(s):
        return {"dp": yh * NX + (x + s) % NX}

    def at_z(s):
        return {"tensor": yl * (NZ * NC) + ((z + s) % NZ) * NC + c}

    y_hi = {"dp": (1 - yh) * NX + x}
    y_lo = {"tensor": (1 - yl) * (NZ * NC) + z * NC + c}
    core = {"tensor": t + 1 - 2 * c}

    loads = [
        pltpu.make_async_copy(tok_hbm, acts.at[0, pl.ds(0, OWN)], local_sem.at[0]),
        pltpu.make_async_copy(cot_hbm, acts.at[1, pl.ds(0, OWN)], local_sem.at[1]),
        pltpu.make_async_copy(win_hbm, win, local_sem.at[2]),
        pltpu.make_async_copy(wout_hbm, wout, local_sem.at[3]),
    ]
    for load in loads:
        load.start()

    barrier = pltpu.get_barrier_semaphore()
    partners = [at_x(s) for s in (1, 2, 3)] + [y_hi, y_lo, core]
    partners += [at_z(s) for s in range(1, NZ)]
    for partner in partners:
        pl.semaphore_signal(barrier, inc=1, device_id=partner, device_id_type=MESH)
    pl.semaphore_wait(barrier, len(partners))

    messages = {}

    def send(key, src, dst, to):
        i = len(messages)
        messages[key] = pltpu.make_async_remote_copy(
            src_ref=src,
            dst_ref=dst,
            send_sem=send_sem.at[i],
            recv_sem=recv_sem.at[i],
            device_id=to,
            device_id_type=MESH,
        )
        messages[key].start()

    def arrived(*key):
        messages[key].wait_recv()

    def rows_at(b, ry, rc, k=0):
        return b * RB + ry * (RB // 2) + rc * (RB // 4) + k * OWN

    def gather_z(s):
        loads[s].wait()
        for b in range(NB):
            for k, o in enumerate(OFFSETS[b]):
                if o:
                    send(
                        ("gz", s, b, k),
                        acts.at[s, pl.ds(0, OWN)],
                        acts.at[s, pl.ds(rows_at(b, 0, 0, k), OWN)],
                        at_z(-o + NZ),
                    )

    def gather_y(b, s):
        for k, o in enumerate(OFFSETS[b]):
            if o:
                arrived("gz", s, b, k)
        n = KO * OWN
        src = acts.at[s, pl.ds(rows_at(b, 0, 0), n)]
        send(("gy", s, b), src, acts.at[s, pl.ds(rows_at(b, 1, 0), n)], y_lo)
        send(("gc", s, b, 0), src, acts.at[s, pl.ds(rows_at(b, 0, 1), n)], core)

    def gather_c(b, s):
        n = KO * OWN
        arrived("gy", s, b)
        src = acts.at[s, pl.ds(rows_at(b, 1, 0), n)]
        send(("gc", s, b, 1), src, acts.at[s, pl.ds(rows_at(b, 1, 1), n)], core)

    def x_rows(b, xi):
        return pl.ds(pl.multiple_of(b * RB + xi * XR, XR), XR)

    def own_rows(b, xi, yi):
        return pl.ds(pl.multiple_of(b * RB + xi * XR + yi * YR, YR), YR)

    def first_product(b, s):
        arrived("gc", s, b, 0)
        arrived("gc", s, b, 1)
        if s == 0 and b < 2:
            loads[2 + b].wait()
        left = acts[s, pl.ds(b * RB, RB), :]
        for n in range(0, W, TN):
            if s == 0:
                part[:, pl.ds(n, TN)] = jnp.dot(
                    left, win[:, pl.ds(n, TN)], preferred_element_type=jnp.float32
                )
            else:
                part[:, pl.ds(n, TN)] = lax.dot_general(
                    left, wout[pl.ds(n, TN), :], (((1,), (1,)), ((), ())),
                    preferred_element_type=jnp.float32,
                )
        sendp[s, pl.ds(b * RB, RB), :] = part[...].astype(jnp.bfloat16)
        for h in (2, 1, 3):
            send(
                ("rx", s, b, h),
                sendp.at[s, x_rows(b, (x + h) % NX)],
                xrecv.at[s, b, h - 1],
                at_x(h),
            )
        ownp[s, b] = part[pl.ds(pl.multiple_of(x * XR, XR), XR), :]

    def reduce_x(b, s):
        for h in (1, 2, 3):
            arrived("rx", s, b, h)
        total = ownp[s, b]
        for h in range(3):
            total = total + xrecv[s, b, h].astype(jnp.float32)
        ownp[s, b] = total
        other = ownp[s, b, pl.ds(pl.multiple_of((1 - yh) * YR, YR), YR), :]
        ysend[s, b] = other.astype(jnp.bfloat16)
        send(("ry", s, b), ysend.at[s, b], yrecv.at[s, b], y_hi)

    def middle(b, s):
        arrived("ry", s, b)
        mine = ownp[s, b, pl.ds(pl.multiple_of(yh * YR, YR), YR), :]
        total = mine + yrecv[s, b].astype(jnp.float32)
        if s == 0:
            value = gelu_value(total)
            slopes[b] = gelu_slope(total)
        else:
            value = total * slopes[b]
        rows = own_rows(b, x, yh)
        mids[s, rows, :] = value.astype(jnp.bfloat16)
        here = mids.at[s, rows]
        send(("ay", s, b), here, here, y_hi)
        for h in (2, 1, 3):
            send(("ax", s, b, h), here, here, at_x(h))

    def forward(b, s):
        arrived("ay", s, b)
        here = mids.at[s, own_rows(b, x, 1 - yh)]
        for h in (2, 1, 3):
            send(("af", s, b, h), here, here, at_x(h))

    def second_product(b, s):
        for h in (1, 2, 3):
            arrived("ax", s, b, h)
            arrived("af", s, b, h)
        left = mids[s, pl.ds(b * RB, RB), :]
        for n in range(0, W, TN):
            if s == 0:
                tens_part[:, pl.ds(n, TN)] = jnp.dot(
                    left, wout[:, pl.ds(n, TN)], preferred_element_type=jnp.float32
                )
            else:
                tens_part[:, pl.ds(n, TN)] = lax.dot_general(
                    left, win[pl.ds(n, TN), :], (((1,), (1,)), ((), ())),
                    preferred_element_type=jnp.float32,
                )
        q = RB // 4
        for ry in range(2):
            core_send[s, b, ry] = tens_part[pl.ds(rows_at(0, ry, 1), q), :]
            core_recv[s, b, 2 + ry] = tens_part[pl.ds(rows_at(0, ry, 0), q), :]
        send(("oc", s, b), core_send.at[s, b], core_recv.at[s, b, pl.ds(0, 2)], core)

    def reduce_c(b, s):
        arrived("oc", s, b)
        ylo_send[s, b] = (core_recv[s, b, 1] + core_recv[s, b, 3]).astype(jnp.bfloat16)
        core_recv[s, b, 2] = core_recv[s, b, 0] + core_recv[s, b, 2]
        send(("oy", s, b), ylo_send.at[s, b], ylo_recv.at[s, b], y_lo)

    def reduce_y(b, s):
        arrived("oy", s, b)
        total = core_recv[s, b, 2] + ylo_recv[s, b].astype(jnp.float32)
        for k, o in enumerate(OFFSETS[b]):
            rows = total[k * OWN : (k + 1) * OWN]
            if o == 0:
                fin_own[s] = rows
            else:
                zsend[s, o] = rows.astype(jnp.bfloat16)
                send(("oz", s, o), zsend.at[s, o], zrecv.at[s, o], at_z(o))

    def finish(s):
        total = fin_own[s]
        for o in range(1, NZ):
            arrived("oz", s, o)
            total = total + zrecv[s, o].astype(jnp.float32)
        if s == 0:
            out_ref[...] = total.astype(jnp.bfloat16)
        else:
            ing_ref[...] = total.astype(jnp.bfloat16)

    gather_z(0)
    gather_z(1)
    items = [(b, s) for s in range(2) for b in range(NB)]
    stages = [
        lambda b, s: gather_y(b, s),
        lambda b, s: gather_c(b, s),
        first_product,
        reduce_x,
        middle,
        forward,
        second_product,
        reduce_c,
        reduce_y,
    ]
    saves = []

    def save(src, dst):
        saves.append(pltpu.make_async_copy(src, dst, local_sem.at[4 + len(saves)]))
        saves[-1].start()

    n_items, n_stages = len(items), len(stages)
    for slot in range(n_items + n_stages - 1):
        for k in reversed(range(n_stages)):
            i = slot - k
            if 0 <= i < n_items:
                b, s = items[i]
                stages[k](b, s)
                if k == 2 and b == NB - 1:
                    save(acts.at[s], (t_out, c_out)[s])
                if k == 6 and b == NB - 1:
                    save(mids.at[s], (a_out, g_out)[s])
    finish(0)
    finish(1)
    for copy in saves:
        copy.wait()
    for copy in messages.values():
        copy.wait_send()


def block(tokens, w_in, w_out, cotangent):
    bf16, f32 = jnp.bfloat16, jnp.float32
    any_space = pl.BlockSpec(memory_space=pl.ANY)
    vmem = pl.BlockSpec(memory_space=pltpu.VMEM)
    wide = jax.ShapeDtypeStruct((ROWS, W), bf16)
    own = jax.ShapeDtypeStruct((OWN, W), bf16)
    q = RB // 4
    return pl.pallas_call(
        block_kernel,
        out_shape=(own, own, wide, wide, wide, wide),
        in_specs=[any_space] * 4,
        out_specs=(vmem, vmem) + (any_space,) * 4,
        scratch_shapes=[
            pltpu.VMEM((W, W), bf16),
            pltpu.VMEM((W, W), bf16),
            pltpu.VMEM((2, ROWS, W), bf16),
            pltpu.VMEM((RB, W), f32),
            pltpu.VMEM((2, ROWS, W), bf16),
            pltpu.VMEM((2, NB, 3, XR, W), bf16),
            pltpu.VMEM((2, NB, YR, W), bf16),
            pltpu.VMEM((2, NB, YR, W), bf16),
            pltpu.VMEM((2, NB, XR, W), f32),
            pltpu.VMEM((NB, YR, W), f32),
            pltpu.VMEM((2, ROWS, W), bf16),
            pltpu.VMEM((2, NB, 2, q, W), f32),
            pltpu.VMEM((2, NB, 4, q, W), f32),
            pltpu.VMEM((RB, W), f32),
            pltpu.VMEM((2, NB, q, W), bf16),
            pltpu.VMEM((2, NB, q, W), bf16),
            pltpu.VMEM((2, OWN, W), f32),
            pltpu.VMEM((2, NZ, OWN, W), bf16),
            pltpu.VMEM((2, NZ, OWN, W), bf16),
            pltpu.SemaphoreType.DMA((8,)),
            pltpu.SemaphoreType.DMA((N_MSG,)),
            pltpu.SemaphoreType.DMA((N_MSG,)),
        ],
        compiler_params=pltpu.CompilerParams(
            collective_id=0, has_side_effects=True, vmem_limit_bytes=56 << 20
        ),
        cost_estimate=pl.CostEstimate(
            flops=8 * ROWS * W * W, bytes_accessed=10 << 20, transcendentals=0
        ),
        name="mlp_block",
    )(tokens, w_in, w_out, cotangent)


def weight_grads_kernel(t_ref, g_ref, a_ref, c_ref, win_grad, wout_grad):
    for left, right, out in ((t_ref, g_ref, win_grad), (a_ref, c_ref, wout_grad)):
        out[...] = lax.dot_general(
            left[...], right[...], (((0,), (0,)), ((), ())),
            preferred_element_type=jnp.float32,
        ).astype(jnp.bfloat16)


def weight_grads(t, g, a, c):
    tm = 128
    whole = pl.BlockSpec((ROWS, W), lambda i: (0, 0))
    piece = pl.BlockSpec((ROWS, tm), lambda i: (0, i))
    out = pl.BlockSpec((tm, W), lambda i: (i, 0))
    return pl.pallas_call(
        weight_grads_kernel,
        grid=(W // tm,),
        out_shape=(jax.ShapeDtypeStruct((W, W), jnp.bfloat16),) * 2,
        in_specs=[piece, whole, piece, whole],
        out_specs=(out, out),
        compiler_params=pltpu.CompilerParams(vmem_limit_bytes=32 << 20),
        name="weight_grads",
    )(t, g, a, c)


def on_device(tokens, w_in, w_out, cotangent):
    output, input_grad, t, c, a, g = block(tokens, w_in, w_out, cotangent)
    w_in_grad, w_out_grad = weight_grads(t, g, a, c)
    return (output, input_grad, w_in_grad, w_out_grad)


def solution(mesh):
    in_specs = (P("tensor", "dp"), P("dp", "tensor"), P("tensor", "dp"), P("tensor", "dp"))
    out_specs = (P("tensor", "dp"), P("tensor", "dp"), P("dp", "tensor"), P("tensor", "dp"))
    return jax.shard_map(
        on_device, mesh=mesh, in_specs=in_specs, out_specs=out_specs, check_vma=False
    )
```

```python
import functools
import math

import jax
import jax.numpy as jnp
from jax import lax
from jax.experimental import pallas as pl
from jax.experimental.pallas import tpu as pltpu
from jax.sharding import PartitionSpec as P

MESH = pl.DeviceIdType.MESH
ROWS = 512
W = 1152
OWN = 16
NX, NYH, NYL, NZ, NC = 4, 2, 2, 8, 2
NB = 4
RB = ROWS // NB
KO = NZ // NB
XR = RB // NX
YR = XR // NYH
OFFSETS = [[0, 1], [7, 2], [6, 3], [5, 4]]
Q = RB // 4
TN = 384
TM = 128
N_LAND, N_LEAVE = 95, 13


def gelu_value(v):
    return v * 0.5 * (1.0 + lax.erf(v * (1.0 / math.sqrt(2.0))))


def gelu_slope(v):
    cdf = 0.5 * (1.0 + lax.erf(v * (1.0 / math.sqrt(2.0))))
    return cdf + v * jnp.exp(-0.5 * v * v) * (1.0 / math.sqrt(2.0 * math.pi))

LAG_GATHER_Y, LAG_GATHER_C = -1.5, -0.1
GATHER_Y_1, GATHER_C_1 = -1.5, -0.1
LAG_PASS_ON, LAG_REDUCE_X, LAG_MIDDLE = 1.9, 3.8, 5.7
LAG_FORWARD_Y, LAG_FORWARD_X, LAG_SECOND = 7.6, 9.5, 11.5
LAG_REDUCE_C, LAG_REDUCE_Y = 12.4, 14.3
FINISH_0 = 20.0
GRAD_AT_1 = [15.45 + 0.5 * m for m in range(W // TM)]
GRAD_AT_0 = [19.46] * 3 + [20.5] * 6
GATHER_1 = -0.05
DIRECT_GATHER = {(0, 0), (1, 0)}
DIRECT_REDUCE = {(0, 1)}
DIAGONAL = {
    f % NZ for b, _ in DIRECT_GATHER | DIRECT_REDUCE for o in OFFSETS[b] for f in (o, -o) if o
}


def block_kernel(
    tok_hbm, win_hbm, wout_hbm, cot_hbm,
    out_ref, ing_ref, wing_ref, woutg_ref,
    win, wout, acts, part, sendp, xrecv, ysend, yrecv, ownp, slopes, mids,
    core_send, core_recv, core_own, tens_part, ylo_send, ylo_recv,
    fin_own, zsend, zrecv, local_sem, send_sem, recv_sem,
):
    bf16, f32 = jnp.bfloat16, jnp.float32
    d, t = lax.axis_index("dp"), lax.axis_index("tensor")
    yh, x = d // NX, d % NX
    yl, z, c = t // (NZ * NC), (t // NC) % NZ, t % NC

    def at_x(s):
        return {"dp": yh * NX + (x + s) % NX}

    def at_z(s, ry=0):
        y = yl if ry == 0 else 1 - yl
        return {"tensor": y * (NZ * NC) + ((z + s) % NZ) * NC + c}

    y_hi = {"dp": (1 - yh) * NX + x}
    core = {"tensor": t + 1 - 2 * c}

    loads = [
        pltpu.make_async_copy(tok_hbm, acts.at[0, pl.ds(0, OWN)], local_sem.at[0]),
        pltpu.make_async_copy(cot_hbm, acts.at[1, pl.ds(0, OWN)], local_sem.at[1]),
        pltpu.make_async_copy(win_hbm, win, local_sem.at[2]),
        pltpu.make_async_copy(wout_hbm, wout, local_sem.at[3]),
    ]
    for load in loads:
        load.start()

    barrier = pltpu.get_barrier_semaphore()
    partners = [at_x(1), at_x(3), y_hi, core, at_z(0, 1)]
    partners += [at_z(s) for s in range(1, NZ)]
    partners += [at_z(s, 1) for s in sorted(DIAGONAL)]
    for partner in partners:
        pl.semaphore_signal(barrier, inc=1, device_id=partner, device_id_type=MESH)
    pl.semaphore_wait(barrier, len(partners))

    landing, leaving = {}, {}

    def send(group, src, dst, to, rows, unit=1):
        kind = group[0]
        i = landing.setdefault(group, [len(landing), 0])
        j = leaving.setdefault(kind, [len(leaving), 0])
        i[1] += rows * unit
        j[1] += rows * unit
        pltpu.make_async_remote_copy(
            src_ref=src,
            dst_ref=dst,
            send_sem=send_sem.at[j[0]],
            recv_sem=recv_sem.at[i[0]],
            device_id=to,
            device_id_type=MESH,
        ).start()

    def bytes_of(rows):
        if rows <= ROWS:
            return acts.at[0, pl.ds(0, rows)]
        if rows == 2 * NB * 6 * YR:
            return xrecv
        assert rows == 2 * NB * 4 * Q, rows
        return core_send

    def arrived(*group):
        i, rows = landing[group]
        view = bytes_of(rows)
        pltpu.make_async_remote_copy(
            view, view, send_sem.at[0], recv_sem.at[i], device_id=core, device_id_type=MESH
        ).wait_recv()

    def all_left():
        for i, rows in leaving.values():
            view = bytes_of(rows)
            pltpu.make_async_remote_copy(
                view, view, send_sem.at[i], recv_sem.at[0], device_id=core, device_id_type=MESH
            ).wait_send()

    def rows_at(b, rc, ry, k=0):
        return b * RB + rc * (RB // 2) + ry * (RB // 4) + k * OWN

    def start_gather(s, blocks):
        loads[s].wait()
        src = acts.at[s, pl.ds(0, OWN)]
        for b in blocks:
            for k, o in enumerate(OFFSETS[b]):
                for ry in range(2):
                    if (o or ry) and (ry == 0 or (b, s) in DIRECT_GATHER):
                        dst = acts.at[s, pl.ds(rows_at(b, 0, ry, k), OWN)]
                        send(("gz", s, b), src, dst, at_z(NZ - o, ry), OWN)

    def gather_y(b, s):
        if (b, s) in DIRECT_GATHER:
            return
        arrived("gz", s, b)
        src = acts.at[s, pl.ds(rows_at(b, 0, 0), Q)]
        send(("gy", s, b), src, acts.at[s, pl.ds(rows_at(b, 0, 1), Q)], at_z(0, 1), Q)

    def gather_c(b, s):
        arrived("gz" if (b, s) in DIRECT_GATHER else "gy", s, b)
        src = acts.at[s, pl.ds(rows_at(b, 0, 0), 2 * Q)]
        send(("gc", s, b), src, acts.at[s, pl.ds(rows_at(b, 1, 0), 2 * Q)], core, 2 * Q)

    def half(b, xi, yi):
        return pl.ds(pl.multiple_of(b * RB + xi * XR + yi * YR, YR), YR)

    def first_product(b, s):
        arrived("gc", s, b)
        if s == 0 and b < 2:
            loads[2 + b].wait()
        left = acts[s, pl.ds(b * RB, RB), :]
        for n in range(0, W, TN):
            cols = pl.ds(n, TN)
            if s == 0:
                part[s, b, :, cols] = jnp.dot(left, win[:, cols], preferred_element_type=f32)
            else:
                part[s, b, :, cols] = lax.dot_general(
                    left, wout[cols, :], (((1,), (1,)), ((), ())), preferred_element_type=f32
                )
        sendp[s, pl.ds(b * RB, RB), :] = part[s, b].astype(bf16)

        def send_half(group, xi, yi, slot, to):
            src = sendp.at[s, half(b, xi % NX, yi)]
            send((group, s, b), src, xrecv.at[s, b, slot], to, YR)

        send_half("r1", x + 2, 0, 0, at_x(1))
        send_half("r1", x + 2, 1, 1, at_x(3))
        send_half("r2", x + 1, 1, 2, at_x(1))
        send_half("r2", x + 3, 0, 3, at_x(3))

    def pass_on(b, s):
        arrived("r1", s, b)
        for i, step in ((0, 1), (1, 3)):
            there = (x + step) % NX
            mine = part[s, b, half(0, there, i), :]
            rows = half(b, there, i)
            sendp[s, rows, :] = (mine + xrecv[s, b, i].astype(f32)).astype(bf16)
            send(("r2", s, b), sendp.at[s, rows], xrecv.at[s, b, 4 + i], at_x(step), YR)

    def reduce_x(b, s):
        arrived("r2", s, b)
        for i in range(2):
            near = xrecv[s, b, 3 - i].astype(f32) + xrecv[s, b, 4 + i].astype(f32)
            ownp[s, b, i] = part[s, b, half(0, x, i), :] + near
        ysend[s, b] = ownp[s, b, 1 - yh].astype(bf16)
        send(("ry", s, b), ysend.at[s, b], yrecv.at[s, b], y_hi, YR)

    def middle(b, s):
        arrived("ry", s, b)
        total = ownp[s, b, yh] + yrecv[s, b].astype(f32)
        if s == 0:
            value = gelu_value(total)
            slopes[b] = gelu_slope(total)
        else:
            value = total * slopes[b]
        rows = half(b, x, yh)
        mids[s, rows, :] = value.astype(bf16)
        here = mids.at[s, rows]
        send(("ay", s, b), here, here, y_hi, YR)
        send(("a1", s, b), here, here, at_x(1), YR)
        send(("a3", s, b), here, here, at_x(3), YR)

    def forward_y(b, s):
        arrived("ay", s, b)
        here = mids.at[s, half(b, x, 1 - yh)]
        send(("a3", s, b), here, here, at_x(1), YR)
        send(("a2", s, b), here, here, at_x(3), YR)

    def forward_x(b, s):
        arrived("a1", s, b)
        here = mids.at[s, half(b, (x + 3) % NX, yh)]
        send(("a3", s, b), here, here, at_x(1), YR)
        arrived("a2", s, b)
        here = mids.at[s, half(b, (x + 1) % NX, 1 - yh)]
        send(("a3", s, b), here, here, at_x(3), YR)

    def second_product(b, s):
        arrived("a3", s, b)
        left = mids[s, pl.ds(b * RB, RB), :]
        for n in range(0, W, TN):
            cols = pl.ds(n, TN)
            if s == 0:
                tens_part[:, cols] = jnp.dot(left, wout[:, cols], preferred_element_type=f32)
            else:
                tens_part[:, cols] = lax.dot_general(
                    left, win[cols, :], (((1,), (1,)), ((), ())), preferred_element_type=f32
                )
        core_send[s, b] = tens_part[pl.ds(2 * Q, 2 * Q), :]
        core_own[s, b] = tens_part[pl.ds(0, 2 * Q), :]
        send(("oc", s, b), core_send.at[s, b], core_recv.at[s, b], core, 2 * Q, 2)

    def send_z(s, o, ry, rows):
        i = 2 * o + ry
        zsend[s, i] = rows.astype(bf16)
        send(("oz", s), zsend.at[s, i], zrecv.at[s, i], at_z(o, ry), OWN)
        summed[s].append(i)

    def reduce_c(b, s):
        arrived("oc", s, b)
        total = core_own[s, b] + core_recv[s, b]
        if (b, s) in DIRECT_REDUCE:
            for k, o in enumerate(OFFSETS[b]):
                for ry in range(2):
                    i = ry * Q + k * OWN
                    if o or ry:
                        send_z(s, o, ry, total[i : i + OWN])
                    else:
                        fin_own[s] = total[i : i + OWN]
        else:
            ylo_send[s, b] = total[Q:].astype(bf16)
            send(("oy", s, b), ylo_send.at[s, b], ylo_recv.at[s, b], at_z(0, 1), Q)
            core_own[s, b, pl.ds(0, Q), :] = total[:Q]

    def reduce_y(b, s):
        if (b, s) in DIRECT_REDUCE:
            return
        arrived("oy", s, b)
        total = core_own[s, b, pl.ds(0, Q), :] + ylo_recv[s, b].astype(f32)
        for k, o in enumerate(OFFSETS[b]):
            rows = total[k * OWN : (k + 1) * OWN]
            if o:
                send_z(s, o, 0, rows)
            else:
                fin_own[s] = rows

    summed = [[], []]

    def finish(s):
        arrived("oz", s)
        total = fin_own[s]
        for i in sorted(summed[s]):
            total = total + zrecv[s, i].astype(f32)
        (out_ref, ing_ref)[s][...] = total.astype(bf16)

    def weight_grad(s, m):
        left, right = (acts, mids) if s == 0 else (mids, acts)
        rows = pl.ds(m * TM, TM)
        (wing_ref, woutg_ref)[s][rows, :] = lax.dot_general(
            left[0, :, rows], right[1], (((0,), (0,)), ((), ())), preferred_element_type=f32
        ).astype(bf16)

    items = [(b, 0) for b in range(NB)] + [(b, 1) for b in reversed(range(NB))]
    last = len(items) - 1
    program = [
        (-9, start_gather, (0, range(NB))),
        (GATHER_1, start_gather, (1, reversed(range(NB)))),
        (FINISH_0, finish, (0,)),
    ]
    for i, (b, s) in enumerate(items):
        for stage, lag in (
            (reduce_y, LAG_REDUCE_Y), (reduce_c, LAG_REDUCE_C), (second_product, LAG_SECOND),
            (forward_x, LAG_FORWARD_X), (forward_y, LAG_FORWARD_Y), (middle, LAG_MIDDLE),
            (reduce_x, LAG_REDUCE_X), (pass_on, LAG_PASS_ON), (first_product, 0.0),
            (gather_c, (LAG_GATHER_C, GATHER_C_1)[s]), (gather_y, (LAG_GATHER_Y, GATHER_Y_1)[s]),
        ):
            program.append((i + lag, stage, (b, s)))
    for m in range(W // TM):
        program.append((GRAD_AT_1[m], weight_grad, (1, m)))
        program.append((GRAD_AT_0[m], weight_grad, (0, m)))
    for _, stage, args in sorted(program, key=lambda entry: entry[0]):
        stage(*args)
    finish(1)
    all_left()
    assert (len(landing), len(leaving)) == (N_LAND, N_LEAVE), (len(landing), len(leaving))


def block(tokens, w_in, w_out, cotangent):
    bf16, f32 = jnp.bfloat16, jnp.float32
    hbm = pl.BlockSpec(memory_space=pltpu.HBM)
    vmem = pl.BlockSpec(memory_space=pltpu.VMEM)
    weight = pltpu.VMEM((W, W), bf16)
    own = pltpu.VMEM((OWN, W), bf16)
    return pl.pallas_call(
        block_kernel,
        out_shape=(own, own, weight, weight),
        in_specs=[hbm] * 4,
        out_specs=(vmem,) * 4,
        scratch_shapes=[
            pltpu.VMEM((W, W), bf16),
            pltpu.VMEM((W, W), bf16),
            pltpu.VMEM((2, ROWS, W), bf16),
            pltpu.VMEM((2, NB, RB, W), f32),
            pltpu.VMEM((2, ROWS, W), bf16),
            pltpu.VMEM((2, NB, 6, YR, W), bf16),
            pltpu.VMEM((2, NB, YR, W), bf16),
            pltpu.VMEM((2, NB, YR, W), bf16),
            pltpu.VMEM((2, NB, 2, YR, W), f32),
            pltpu.VMEM((NB, YR, W), f32),
            pltpu.VMEM((2, ROWS, W), bf16),
            pltpu.VMEM((2, NB, 2 * Q, W), f32),
            pltpu.VMEM((2, NB, 2 * Q, W), f32),
            pltpu.VMEM((2, NB, 2 * Q, W), f32),
            pltpu.VMEM((RB, W), f32),
            pltpu.VMEM((2, NB, Q, W), bf16),
            pltpu.VMEM((2, NB, Q, W), bf16),
            pltpu.VMEM((2, OWN, W), f32),
            pltpu.VMEM((2, NZ * 2, OWN, W), bf16),
            pltpu.VMEM((2, NZ * 2, OWN, W), bf16),
            pltpu.SemaphoreType.DMA((4,)),
            pltpu.SemaphoreType.DMA((N_LEAVE,)),
            pltpu.SemaphoreType.DMA((N_LAND,)),
        ],
        compiler_params=pltpu.CompilerParams(
            collective_id=0, has_side_effects=True, vmem_limit_bytes=42 << 20
        ),
        cost_estimate=pl.CostEstimate(
            flops=12 * ROWS * W * W, bytes_accessed=12 << 20, transcendentals=0
        ),
        name="mlp_block",
    )(tokens, w_in, w_out, cotangent)


def on_device(tokens, w_in, w_out, cotangent):
    args = [pltpu.with_memory_space_constraint(a, pltpu.HBM) for a in (tokens, w_in, w_out, cotangent)]
    return block(*args)


def solution(mesh):
    in_specs = (P("tensor", "dp"), P("dp", "tensor"), P("tensor", "dp"), P("tensor", "dp"))
    out_specs = (P("tensor", "dp"), P("tensor", "dp"), P("dp", "tensor"), P("tensor", "dp"))
    return jax.shard_map(
        on_device, mesh=mesh, in_specs=in_specs, out_specs=out_specs, check_vma=False
    )
```

```python
import math

import jax
import jax.numpy as jnp
from jax import lax
from jax.experimental import pallas as pl
from jax.experimental.pallas import tpu as pltpu
from jax.sharding import PartitionSpec as P

MESH = pl.DeviceIdType.MESH
ROWS = 512
W = 1152
OWN = 16
NX, NYH, NYL, NZ, NC = 4, 2, 2, 8, 2
NB = 4
RB = ROWS // NB
KO = NZ // NB
XR = RB // NX
YR = XR // NYH
OFFSETS = [[0, 1], [7, 2], [6, 3], [5, 4]]
Q = RB // 4
TN = 384
STORE_ROWS = 288
TM = 128
N_LEAVE = 13


def gelu_value(v):
    return v * 0.5 * (1.0 + lax.erf(v * (1.0 / math.sqrt(2.0))))


def gelu_slope(v):
    cdf = 0.5 * (1.0 + lax.erf(v * (1.0 / math.sqrt(2.0))))
    return cdf + v * jnp.exp(-0.5 * v * v) * (1.0 / math.sqrt(2.0 * math.pi))

ORDER = [
    ("sg", 0, 0), ("sg", 1, 0), ("sg", 2, 0), ("sg", 3, 0), ("gy", 0, 0), ("gy", 1, 0),
    ("gy", 2, 0), ("sg", 2, 1), ("gc", 0, 0), ("gy", 3, 0), ("sg", 3, 1), ("p1", 0, 0),
    ("gc", 1, 0), ("sg", 1, 1), ("sg", 0, 1), ("gc", 2, 0), ("p1", 1, 0), ("p1", 2, 0),
    ("gc", 3, 0), ("gy", 2, 1), ("po", 0, 0), ("p1", 3, 0), ("gy", 1, 1), ("gy", 0, 1),
    ("po", 1, 0), ("gy", 3, 1), ("po", 2, 0), ("gc", 2, 1), ("p1", 2, 1), ("gc", 1, 1),
    ("po", 3, 0), ("rx", 0, 0), ("gc", 0, 1), ("p1", 1, 1), ("rx", 1, 0), ("rx", 2, 0),
    ("p1", 0, 1), ("gc", 3, 1), ("po", 2, 1), ("mi", 0, 0), ("p1", 3, 1), ("rx", 3, 0),
    ("po", 1, 1), ("mi", 1, 0), ("mi", 2, 0), ("po", 0, 1), ("fy", 0, 0), ("rx", 2, 1),
    ("fr", 0, 0), ("mi", 3, 0), ("po", 3, 1), ("fy", 1, 0), ("fy", 2, 0), ("rx", 1, 1),
    ("fr", 1, 0), ("mi", 2, 1), ("fr", 2, 0), ("rx", 0, 1), ("fy", 3, 0), ("fl", 0, 0),
    ("mi", 1, 1), ("fr", 3, 0), ("rx", 3, 1), ("fl", 1, 0), ("fy", 2, 1), ("fl", 2, 0),
    ("mi", 0, 1), ("fl", 3, 0), ("fr", 2, 1), ("p2", 0, 0), ("fy", 1, 1), ("mi", 3, 1),
    ("p2", 1, 0), ("rc", 0, 0), ("fl", 2, 1), ("fr", 1, 1), ("fy", 0, 1), ("p2", 2, 0),
    ("rc", 1, 0), ("fr", 0, 1), ("p2", 3, 0), ("rc", 2, 0), ("fl", 1, 1), ("wg", 0, 1),
    ("fy", 3, 1), ("wg", 1, 1), ("wg", 2, 1), ("wg", 3, 1), ("ry", 0, 0), ("fr", 3, 1),
    ("rc", 3, 0), ("p2", 2, 1), ("fl", 0, 1), ("wg", 4, 1), ("ry", 1, 0), ("wg", 5, 1),
    ("wg", 6, 1), ("p2", 1, 1), ("ry", 2, 0), ("fl", 3, 1), ("rc", 2, 1), ("wg", 7, 1),
    ("wg", 8, 1), ("ry", 3, 0), ("p2", 0, 1), ("rc", 1, 1), ("p2", 3, 1), ("ry", 2, 1),
    ("rc", 0, 1), ("rc", 3, 1), ("ry", 1, 1), ("fi", 0), ("ry", 3, 1), ("wg", 0, 0), ("wg", 1, 0),
    ("wg", 2, 0), ("wg", 3, 0), ("wg", 4, 0), ("wg", 5, 0), ("wg", 6, 0), ("wg", 7, 0),
    ("wg", 8, 0), ("fi", 1),
]
DIRECT_GATHER = set()
DIRECT_REDUCE = {(0, 1)}
N_LAND = 2 + 12 * 2 * NB - len(DIRECT_GATHER) - len(DIRECT_REDUCE)
DIAGONAL = {
    f % NZ for b, _ in DIRECT_GATHER | DIRECT_REDUCE for o in OFFSETS[b] for f in (o, -o) if o
}


def block_kernel(
    tok_hbm, win_hbm, wout_hbm, cot_hbm,
    out_ref, ing_ref, wing_ref, woutg_ref,
    win, wout, acts, part, sendp, xrecv, ysend, yrecv, ownp, slopes, mids,
    core_send, core_recv, core_own, tens_part, ylo_send, ylo_recv,
    fin_own, zsend, zrecv, local_sem, send_sem, recv_sem,
):
    bf16, f32 = jnp.bfloat16, jnp.float32
    d, t = lax.axis_index("dp"), lax.axis_index("tensor")
    yh, x = d // NX, d % NX
    yl, z, c = t // (NZ * NC), (t // NC) % NZ, t % NC

    def at_x(s):
        return {"dp": yh * NX + (x + s) % NX}

    def at_z(s, ry=0):
        y = yl if ry == 0 else 1 - yl
        return {"tensor": y * (NZ * NC) + ((z + s) % NZ) * NC + c}

    y_hi = {"dp": (1 - yh) * NX + x}
    core = {"tensor": t + 1 - 2 * c}

    loads = [
        pltpu.make_async_copy(tok_hbm, acts.at[0, pl.ds(0, OWN)], local_sem.at[0]),
        pltpu.make_async_copy(cot_hbm, acts.at[1, pl.ds(0, OWN)], local_sem.at[1]),
        pltpu.make_async_copy(win_hbm, win, local_sem.at[2]),
        pltpu.make_async_copy(wout_hbm, wout, local_sem.at[3]),
    ]
    for load in loads:
        load.start()

    barrier = pltpu.get_barrier_semaphore()
    partners = [at_x(1), at_x(3), y_hi, core, at_z(0, 1)]
    partners += [at_z(s) for s in range(1, NZ)]
    partners += [at_z(s, 1) for s in sorted(DIAGONAL)]
    for partner in partners:
        pl.semaphore_signal(barrier, inc=1, device_id=partner, device_id_type=MESH)
    pl.semaphore_wait(barrier, len(partners))

    landing, leaving = {}, {}

    def send(group, src, dst, to, rows, unit=1):
        kind = group[0]
        i = landing.setdefault(group, [len(landing), 0])
        j = leaving.setdefault(kind, [len(leaving), 0])
        i[1] += rows * unit
        j[1] += rows * unit
        pltpu.make_async_remote_copy(
            src_ref=src,
            dst_ref=dst,
            send_sem=send_sem.at[j[0]],
            recv_sem=recv_sem.at[i[0]],
            device_id=to,
            device_id_type=MESH,
        ).start()

    def bytes_of(rows):
        if rows <= ROWS:
            return acts.at[0, pl.ds(0, rows)]
        if rows == 2 * NB * 6 * YR:
            return xrecv
        assert rows == 2 * NB * 4 * Q, rows
        return core_send

    def arrived(*group):
        i, rows = landing[group]
        view = bytes_of(rows)
        pltpu.make_async_remote_copy(
            view, view, send_sem.at[0], recv_sem.at[i], device_id=core, device_id_type=MESH
        ).wait_recv()

    def all_left():
        for i, rows in leaving.values():
            view = bytes_of(rows)
            pltpu.make_async_remote_copy(
                view, view, send_sem.at[i], recv_sem.at[0], device_id=core, device_id_type=MESH
            ).wait_send()

    def rows_at(b, rc, ry, k=0):
        return b * RB + rc * (RB // 2) + ry * (RB // 4) + k * OWN

    def start_gather(b, s):
        src = acts.at[s, pl.ds(0, OWN)]
        for k, o in enumerate(OFFSETS[b]):
            for ry in range(2):
                if (o or ry) and (ry == 0 or (b, s) in DIRECT_GATHER):
                    dst = acts.at[s, pl.ds(rows_at(b, 0, ry, k), OWN)]
                    send(("gz", s, b), src, dst, at_z(NZ - o, ry), OWN)

    def gather_y(b, s):
        if (b, s) in DIRECT_GATHER:
            return
        arrived("gz", s, b)
        src = acts.at[s, pl.ds(rows_at(b, 0, 0), Q)]
        send(("gy", s, b), src, acts.at[s, pl.ds(rows_at(b, 0, 1), Q)], at_z(0, 1), Q)

    def gather_c(b, s):
        arrived("gz" if (b, s) in DIRECT_GATHER else "gy", s, b)
        src = acts.at[s, pl.ds(rows_at(b, 0, 0), 2 * Q)]
        send(("gc", s, b), src, acts.at[s, pl.ds(rows_at(b, 1, 0), 2 * Q)], core, 2 * Q)

    def half(b, xi, yi):
        return pl.ds(pl.multiple_of(b * RB + xi * XR + yi * YR, YR), YR)

    def first_product(b, s):
        arrived("gc", s, b)
        if s == 0 and b < 2:
            loads[2 + b].wait()
        left = acts[s, pl.ds(b * RB, RB), :]
        for n in range(0, W, TN):
            cols = pl.ds(n, TN)
            if s == 0:
                part[s, b, :, cols] = jnp.dot(left, win[:, cols], preferred_element_type=f32)
            else:
                part[s, b, :, cols] = lax.dot_general(
                    left, wout[cols, :], (((1,), (1,)), ((), ())), preferred_element_type=f32
                )
        sendp[s, pl.ds(b * RB, RB), :] = part[s, b].astype(bf16)

        def send_half(group, xi, yi, slot, to):
            src = sendp.at[s, half(b, xi % NX, yi)]
            send((group, s, b), src, xrecv.at[s, b, slot], to, YR)

        send_half("r1", x + 2, 0, 0, at_x(1))
        send_half("r1", x + 2, 1, 1, at_x(3))
        send_half("r2", x + 1, 1, 2, at_x(1))
        send_half("r2", x + 3, 0, 3, at_x(3))

    def pass_on(b, s):
        arrived("r1", s, b)
        for i, step in ((0, 1), (1, 3)):
            there = (x + step) % NX
            mine = part[s, b, half(0, there, i), :]
            rows = half(b, there, i)
            sendp[s, rows, :] = (mine + xrecv[s, b, i].astype(f32)).astype(bf16)
            send(("r2", s, b), sendp.at[s, rows], xrecv.at[s, b, 4 + i], at_x(step), YR)

    def reduce_x(b, s):
        arrived("r2", s, b)
        for i in range(2):
            near = xrecv[s, b, 3 - i].astype(f32) + xrecv[s, b, 4 + i].astype(f32)
            ownp[s, b, i] = part[s, b, half(0, x, i), :] + near
        ysend[s, b] = ownp[s, b, 1 - yh].astype(bf16)
        send(("ry", s, b), ysend.at[s, b], yrecv.at[s, b], y_hi, YR)

    def middle(b, s):
        arrived("ry", s, b)
        total = ownp[s, b, yh] + yrecv[s, b].astype(f32)
        if s == 0:
            value = gelu_value(total)
            slopes[b] = gelu_slope(total)
        else:
            value = total * slopes[b]
        rows = half(b, x, yh)
        mids[s, rows, :] = value.astype(bf16)
        here = mids.at[s, rows]
        send(("ay", s, b), here, here, y_hi, YR)
        send(("a1", s, b), here, here, at_x(1), YR)
        send(("a3", s, b), here, here, at_x(3), YR)

    def forward_y(b, s):
        arrived("ay", s, b)
        here = mids.at[s, half(b, x, 1 - yh)]
        send(("a3", s, b), here, here, at_x(1), YR)
        send(("a2", s, b), here, here, at_x(3), YR)

    def forward_right(b, s):
        arrived("a1", s, b)
        here = mids.at[s, half(b, (x + 3) % NX, yh)]
        send(("a3", s, b), here, here, at_x(1), YR)

    def forward_left(b, s):
        arrived("a2", s, b)
        here = mids.at[s, half(b, (x + 1) % NX, 1 - yh)]
        send(("a3", s, b), here, here, at_x(3), YR)

    def second_product(b, s):
        arrived("a3", s, b)
        left = mids[s, pl.ds(b * RB, RB), :]
        for n in range(0, W, TN):
            cols = pl.ds(n, TN)
            if s == 0:
                tens_part[:, cols] = jnp.dot(left, wout[:, cols], preferred_element_type=f32)
            else:
                tens_part[:, cols] = lax.dot_general(
                    left, win[cols, :], (((1,), (1,)), ((), ())), preferred_element_type=f32
                )
        core_send[s, b] = tens_part[pl.ds(2 * Q, 2 * Q), :]
        core_own[s, b] = tens_part[pl.ds(0, 2 * Q), :]
        send(("oc", s, b), core_send.at[s, b], core_recv.at[s, b], core, 2 * Q, 2)

    def send_z(s, o, ry, rows):
        i = 2 * o + ry
        zsend[s, i] = rows.astype(bf16)
        send(("oz", s), zsend.at[s, i], zrecv.at[s, i], at_z(o, ry), OWN)
        summed[s].append(i)

    def reduce_c(b, s):
        arrived("oc", s, b)
        total = core_own[s, b] + core_recv[s, b]
        if (b, s) in DIRECT_REDUCE:
            for k, o in enumerate(OFFSETS[b]):
                for ry in range(2):
                    i = ry * Q + k * OWN
                    if o or ry:
                        send_z(s, o, ry, total[i : i + OWN])
                    else:
                        fin_own[s] = total[i : i + OWN]
        else:
            ylo_send[s, b] = total[Q:].astype(bf16)
            send(("oy", s, b), ylo_send.at[s, b], ylo_recv.at[s, b], at_z(0, 1), Q)
            core_own[s, b, pl.ds(0, Q), :] = total[:Q]

    def reduce_y(b, s):
        if (b, s) in DIRECT_REDUCE:
            return
        arrived("oy", s, b)
        total = core_own[s, b, pl.ds(0, Q), :] + ylo_recv[s, b].astype(f32)
        for k, o in enumerate(OFFSETS[b]):
            rows = total[k * OWN : (k + 1) * OWN]
            if o:
                send_z(s, o, 0, rows)
            else:
                fin_own[s] = rows

    summed = [[], []]

    def finish(s):
        arrived("oz", s)
        total = fin_own[s]
        for i in sorted(summed[s]):
            total = total + zrecv[s, i].astype(f32)
        (out_ref, ing_ref)[s][...] = total.astype(bf16)

    def weight_grad(m, s):
        left, right = (acts, mids) if s == 0 else (mids, acts)
        rows = pl.ds(m * TM, TM)
        (wing_ref, woutg_ref)[s][rows, :] = lax.dot_general(
            left[0, :, rows], right[1], (((0,), (0,)), ((), ())), preferred_element_type=f32
        ).astype(bf16)

    stages = {
        "sg": start_gather, "gy": gather_y, "gc": gather_c, "p1": first_product,
        "po": pass_on, "rx": reduce_x, "mi": middle, "fy": forward_y, "fr": forward_right,
        "fl": forward_left, "p2": second_product, "rc": reduce_c, "ry": reduce_y,
        "wg": weight_grad, "fi": finish,
    }
    for load in loads[:2]:
        load.wait()
    for name, *args in ORDER:
        stages[name](*args)
    all_left()
    assert (len(landing), len(leaving)) == (N_LAND, N_LEAVE), (len(landing), len(leaving))


def block(tokens, w_in, w_out, cotangent):
    bf16, f32 = jnp.bfloat16, jnp.float32
    hbm = pl.BlockSpec(memory_space=pltpu.HBM)
    vmem = pl.BlockSpec(memory_space=pltpu.VMEM)
    weight = pltpu.VMEM((W, W), bf16)
    own = pltpu.VMEM((OWN, W), bf16)
    return pl.pallas_call(
        block_kernel,
        out_shape=(own, own, weight, weight),
        in_specs=[hbm] * 4,
        out_specs=(vmem,) * 4,
        scratch_shapes=[
            pltpu.VMEM((W, W), bf16),
            pltpu.VMEM((W, W), bf16),
            pltpu.VMEM((2, ROWS, W), bf16),
            pltpu.VMEM((2, NB, RB, W), f32),
            pltpu.VMEM((2, ROWS, W), bf16),
            pltpu.VMEM((2, NB, 6, YR, W), bf16),
            pltpu.VMEM((2, NB, YR, W), bf16),
            pltpu.VMEM((2, NB, YR, W), bf16),
            pltpu.VMEM((2, NB, 2, YR, W), f32),
            pltpu.VMEM((NB, YR, W), f32),
            pltpu.VMEM((2, ROWS, W), bf16),
            pltpu.VMEM((2, NB, 2 * Q, W), f32),
            pltpu.VMEM((2, NB, 2 * Q, W), f32),
            pltpu.VMEM((2, NB, 2 * Q, W), f32),
            pltpu.VMEM((RB, W), f32),
            pltpu.VMEM((2, NB, Q, W), bf16),
            pltpu.VMEM((2, NB, Q, W), bf16),
            pltpu.VMEM((2, OWN, W), f32),
            pltpu.VMEM((2, NZ * 2, OWN, W), bf16),
            pltpu.VMEM((2, NZ * 2, OWN, W), bf16),
            pltpu.SemaphoreType.DMA((4,)),
            pltpu.SemaphoreType.DMA((N_LEAVE,)),
            pltpu.SemaphoreType.DMA((N_LAND,)),
        ],
        compiler_params=pltpu.CompilerParams(
            collective_id=0, has_side_effects=True, vmem_limit_bytes=42 << 20
        ),
        cost_estimate=pl.CostEstimate(
            flops=12 * ROWS * W * W, bytes_accessed=12 << 20, transcendentals=0
        ),
        name="mlp_block",
    )(tokens, w_in, w_out, cotangent)


def store_kernel(*refs):
    n = len(refs) // 2
    sems = refs[-1]
    copies = []
    for source, target in zip(refs[:n], refs[n:-1]):
        for rows in range(0, source.shape[0], STORE_ROWS):
            piece = pl.ds(rows, min(STORE_ROWS, source.shape[0]))
            copies.append(
                pltpu.make_async_copy(source.at[piece], target.at[piece], sems.at[len(copies)])
            )
    for copy in copies:
        copy.start()
    for copy in copies:
        copy.wait()


def store(*arrays):
    hbm = pl.BlockSpec(memory_space=pltpu.HBM)
    return pl.pallas_call(
        store_kernel,
        out_shape=tuple(jax.ShapeDtypeStruct(a.shape, a.dtype) for a in arrays),
        in_specs=[pl.BlockSpec(memory_space=pltpu.VMEM)] * len(arrays),
        out_specs=(hbm,) * len(arrays),
        scratch_shapes=[pltpu.SemaphoreType.DMA((2 + 2 * W // STORE_ROWS,))],
        compiler_params=pltpu.CompilerParams(vmem_limit_bytes=1 << 20),
        name="store",
    )(*arrays)


def on_device(tokens, w_in, w_out, cotangent):
    args = [pltpu.with_memory_space_constraint(a, pltpu.HBM) for a in (tokens, w_in, w_out, cotangent)]
    return store(*block(*args))


def solution(mesh):
    in_specs = (P("tensor", "dp"), P("dp", "tensor"), P("tensor", "dp"), P("tensor", "dp"))
    out_specs = (P("tensor", "dp"), P("tensor", "dp"), P("dp", "tensor"), P("tensor", "dp"))
    return jax.shard_map(
        on_device, mesh=mesh, in_specs=in_specs, out_specs=out_specs, check_vma=False
    )
```

```python
import math

import jax
import jax.numpy as jnp
from jax import lax
from jax.experimental import pallas as pl
from jax.experimental.pallas import tpu as pltpu
from jax.sharding import PartitionSpec as P

MESH = pl.DeviceIdType.MESH
ROWS = 512
W = 1152
OWN = 16
NX, NYH, NYL, NZ, NC = 4, 2, 2, 8, 2
NB = 4
RB = ROWS // NB
KO = NZ // NB
XR = RB // NX
YR = XR // NYH
OFFSETS = [[0, 1], [6, 3], [5, 4], [7, 2]]
Q = RB // 4
TN = 384
STORE_ROWS = 288
TM = 128
N_LEAVE = 13


def gelu_value(v):
    return v * 0.5 * (1.0 + lax.erf(v * (1.0 / math.sqrt(2.0))))


def gelu_slope(v):
    cdf = 0.5 * (1.0 + lax.erf(v * (1.0 / math.sqrt(2.0))))
    return cdf + v * jnp.exp(-0.5 * v * v) * (1.0 / math.sqrt(2.0 * math.pi))

ORDER = [
    ("sg", 0, 0), ("sg", 1, 0), ("sg", 2, 0), ("sg", 3, 0), ("gy", 0, 0), ("gy", 1, 0),
    ("gy", 2, 0), ("sg", 2, 1), ("gc", 0, 0), ("gy", 3, 0), ("sg", 3, 1), ("p1", 0, 0),
    ("gc", 1, 0), ("sg", 1, 1), ("sg", 0, 1), ("gc", 2, 0), ("p1", 1, 0), ("p1", 2, 0),
    ("gc", 3, 0), ("gy", 2, 1), ("po", 0, 0), ("p1", 3, 0), ("gy", 1, 1), ("gy", 0, 1),
    ("po", 1, 0), ("gy", 3, 1), ("po", 2, 0), ("gc", 2, 1), ("p1", 2, 1), ("gc", 1, 1),
    ("po", 3, 0), ("rx", 0, 0), ("gc", 0, 1), ("p1", 1, 1), ("rx", 1, 0), ("rx", 2, 0),
    ("p1", 0, 1), ("gc", 3, 1), ("po", 2, 1), ("mi", 0, 0), ("p1", 3, 1), ("rx", 3, 0),
    ("po", 1, 1), ("mi", 1, 0), ("mi", 2, 0), ("po", 0, 1), ("fy", 0, 0), ("rx", 2, 1),
    ("fr", 0, 0), ("mi", 3, 0), ("po", 3, 1), ("fy", 1, 0), ("fy", 2, 0), ("rx", 1, 1),
    ("fr", 1, 0), ("mi", 2, 1), ("fr", 2, 0), ("rx", 0, 1), ("fy", 3, 0), ("fl", 0, 0),
    ("mi", 1, 1), ("fr", 3, 0), ("rx", 3, 1), ("fl", 1, 0), ("fy", 2, 1), ("fl", 2, 0),
    ("mi", 0, 1), ("fl", 3, 0), ("fr", 2, 1), ("p2", 0, 0), ("fy", 1, 1), ("mi", 3, 1),
    ("p2", 1, 0), ("rc", 0, 0), ("fl", 2, 1), ("fr", 1, 1), ("fy", 0, 1), ("p2", 2, 0),
    ("rc", 1, 0), ("fr", 0, 1), ("p2", 3, 0), ("rc", 2, 0), ("fl", 1, 1), ("wg", 0, 1),
    ("fy", 3, 1), ("wg", 1, 1), ("wg", 2, 1), ("wg", 3, 1), ("ry", 0, 0), ("fr", 3, 1),
    ("rc", 3, 0), ("p2", 2, 1), ("fl", 0, 1), ("wg", 4, 1), ("ry", 1, 0), ("wg", 5, 1),
    ("wg", 6, 1), ("p2", 1, 1), ("ry", 2, 0), ("fl", 3, 1), ("rc", 2, 1), ("wg", 7, 1),
    ("wg", 8, 1), ("ry", 3, 0), ("p2", 0, 1), ("rc", 1, 1), ("p2", 3, 1), ("ry", 2, 1),
    ("rc", 0, 1), ("rc", 3, 1), ("ry", 1, 1), ("ry", 0, 1), ("fi", 0), ("ry", 3, 1), ("wg", 0, 0), ("wg", 1, 0),
    ("wg", 2, 0), ("wg", 3, 0), ("wg", 4, 0), ("wg", 5, 0), ("wg", 6, 0), ("wg", 7, 0),
    ("wg", 8, 0), ("fi", 1),
]
DIRECT_GATHER = set()
DIRECT_REDUCE = set()
N_LAND = 2 + 12 * 2 * NB - len(DIRECT_GATHER) - len(DIRECT_REDUCE)
DIAGONAL = {
    f % NZ for b, _ in DIRECT_GATHER | DIRECT_REDUCE for o in OFFSETS[b] for f in (o, -o) if o
}


def block_kernel(
    tok_hbm, win_hbm, wout_hbm, cot_hbm,
    out_ref, ing_ref, wing_ref, woutg_ref,
    win, wout, acts, part, sendp, xrecv, ysend, yrecv, ownp, slopes, mids,
    core_send, core_recv, core_own, tens_part, ylo_send, ylo_recv,
    fin_own, zsend, zrecv, local_sem, send_sem, recv_sem,
):
    bf16, f32 = jnp.bfloat16, jnp.float32
    d, t = lax.axis_index("dp"), lax.axis_index("tensor")
    yh, x = d // NX, d % NX
    yl, z, c = t // (NZ * NC), (t // NC) % NZ, t % NC

    def at_x(s):
        return {"dp": yh * NX + (x + s) % NX}

    def at_z(s, ry=0):
        y = yl if ry == 0 else 1 - yl
        return {"tensor": y * (NZ * NC) + ((z + s) % NZ) * NC + c}

    y_hi = {"dp": (1 - yh) * NX + x}
    core = {"tensor": t + 1 - 2 * c}

    loads = [
        pltpu.make_async_copy(tok_hbm, acts.at[0, pl.ds(0, OWN)], local_sem.at[0]),
        pltpu.make_async_copy(cot_hbm, acts.at[1, pl.ds(0, OWN)], local_sem.at[1]),
        pltpu.make_async_copy(win_hbm, win, local_sem.at[2]),
        pltpu.make_async_copy(wout_hbm, wout, local_sem.at[3]),
    ]
    for load in loads:
        load.start()

    barrier = pltpu.get_barrier_semaphore()
    partners = [at_x(1), at_x(3), y_hi, core, at_z(0, 1)]
    partners += [at_z(s) for s in range(1, NZ)]
    partners += [at_z(s, 1) for s in sorted(DIAGONAL)]
    for partner in partners:
        pl.semaphore_signal(barrier, inc=1, device_id=partner, device_id_type=MESH)
    pl.semaphore_wait(barrier, len(partners))

    landing, leaving = {}, {}

    def send(group, src, dst, to, rows, unit=1):
        kind = group[0]
        i = landing.setdefault(group, [len(landing), 0])
        j = leaving.setdefault(kind, [len(leaving), 0])
        i[1] += rows * unit
        j[1] += rows * unit
        pltpu.make_async_remote_copy(
            src_ref=src,
            dst_ref=dst,
            send_sem=send_sem.at[j[0]],
            recv_sem=recv_sem.at[i[0]],
            device_id=to,
            device_id_type=MESH,
        ).start()

    def bytes_of(rows):
        if rows <= ROWS:
            return acts.at[0, pl.ds(0, rows)]
        if rows == 2 * NB * 6 * YR:
            return xrecv
        assert rows == 2 * NB * 4 * Q, rows
        return core_send

    def arrived(*group):
        i, rows = landing[group]
        view = bytes_of(rows)
        pltpu.make_async_remote_copy(
            view, view, send_sem.at[0], recv_sem.at[i], device_id=core, device_id_type=MESH
        ).wait_recv()

    def all_left():
        for i, rows in leaving.values():
            view = bytes_of(rows)
            pltpu.make_async_remote_copy(
                view, view, send_sem.at[i], recv_sem.at[0], device_id=core, device_id_type=MESH
            ).wait_send()

    def rows_at(b, rc, ry, k=0):
        return b * RB + rc * (RB // 2) + ry * (RB // 4) + k * OWN

    def start_gather(b, s):
        src = acts.at[s, pl.ds(0, OWN)]
        for k, o in enumerate(OFFSETS[b]):
            for ry in range(2):
                if (o or ry) and (ry == 0 or (b, s) in DIRECT_GATHER):
                    dst = acts.at[s, pl.ds(rows_at(b, 0, ry, k), OWN)]
                    send(("gz", s, b), src, dst, at_z(NZ - o, ry), OWN)

    def gather_y(b, s):
        if (b, s) in DIRECT_GATHER:
            return
        arrived("gz", s, b)
        src = acts.at[s, pl.ds(rows_at(b, 0, 0), Q)]
        send(("gy", s, b), src, acts.at[s, pl.ds(rows_at(b, 0, 1), Q)], at_z(0, 1), Q)

    def gather_c(b, s):
        arrived("gz" if (b, s) in DIRECT_GATHER else "gy", s, b)
        src = acts.at[s, pl.ds(rows_at(b, 0, 0), 2 * Q)]
        send(("gc", s, b), src, acts.at[s, pl.ds(rows_at(b, 1, 0), 2 * Q)], core, 2 * Q)

    def half(b, xi, yi):
        return pl.ds(pl.multiple_of(b * RB + xi * XR + yi * YR, YR), YR)

    def first_product(b, s):
        arrived("gc", s, b)
        if s == 0 and b < 2:
            loads[2 + b].wait()
        left = acts[s, pl.ds(b * RB, RB), :]
        for n in range(0, W, TN):
            cols = pl.ds(n, TN)
            if s == 0:
                part[s, b, :, cols] = jnp.dot(left, win[:, cols], preferred_element_type=f32)
            else:
                part[s, b, :, cols] = lax.dot_general(
                    left, wout[cols, :], (((1,), (1,)), ((), ())), preferred_element_type=f32
                )
        sendp[s, pl.ds(b * RB, RB), :] = part[s, b].astype(bf16)

        def send_half(group, xi, yi, slot, to):
            src = sendp.at[s, half(b, xi % NX, yi)]
            send((group, s, b), src, xrecv.at[s, b, slot], to, YR)

        send_half("r1", x + 2, 0, 0, at_x(1))
        send_half("r1", x + 2, 1, 1, at_x(3))
        send_half("r2", x + 1, 1, 2, at_x(1))
        send_half("r2", x + 3, 0, 3, at_x(3))

    def pass_on(b, s):
        arrived("r1", s, b)
        for i, step in ((0, 1), (1, 3)):
            there = (x + step) % NX
            mine = part[s, b, half(0, there, i), :]
            rows = half(b, there, i)
            sendp[s, rows, :] = (mine + xrecv[s, b, i].astype(f32)).astype(bf16)
            send(("r2", s, b), sendp.at[s, rows], xrecv.at[s, b, 4 + i], at_x(step), YR)

    def reduce_x(b, s):
        arrived("r2", s, b)
        for i in range(2):
            near = xrecv[s, b, 3 - i].astype(f32) + xrecv[s, b, 4 + i].astype(f32)
            ownp[s, b, i] = part[s, b, half(0, x, i), :] + near
        ysend[s, b] = ownp[s, b, 1 - yh].astype(bf16)
        send(("ry", s, b), ysend.at[s, b], yrecv.at[s, b], y_hi, YR)

    def middle(b, s):
        arrived("ry", s, b)
        total = ownp[s, b, yh] + yrecv[s, b].astype(f32)
        if s == 0:
            value = gelu_value(total)
            slopes[b] = gelu_slope(total)
        else:
            value = total * slopes[b]
        rows = half(b, x, yh)
        mids[s, rows, :] = value.astype(bf16)
        here = mids.at[s, rows]
        send(("ay", s, b), here, here, y_hi, YR)
        send(("a1", s, b), here, here, at_x(1), YR)
        send(("a3", s, b), here, here, at_x(3), YR)

    def forward_y(b, s):
        arrived("ay", s, b)
        here = mids.at[s, half(b, x, 1 - yh)]
        send(("a3", s, b), here, here, at_x(1), YR)
        send(("a2", s, b), here, here, at_x(3), YR)

    def forward_right(b, s):
        arrived("a1", s, b)
        here = mids.at[s, half(b, (x + 3) % NX, yh)]
        send(("a3", s, b), here, here, at_x(1), YR)

    def forward_left(b, s):
        arrived("a2", s, b)
        here = mids.at[s, half(b, (x + 1) % NX, 1 - yh)]
        send(("a3", s, b), here, here, at_x(3), YR)

    def second_product(b, s):
        arrived("a3", s, b)
        left = mids[s, pl.ds(b * RB, RB), :]
        for n in range(0, W, TN):
            cols = pl.ds(n, TN)
            if s == 0:
                tens_part[:, cols] = jnp.dot(left, wout[:, cols], preferred_element_type=f32)
            else:
                tens_part[:, cols] = lax.dot_general(
                    left, win[cols, :], (((1,), (1,)), ((), ())), preferred_element_type=f32
                )
        core_send[s, b] = tens_part[pl.ds(2 * Q, 2 * Q), :]
        core_own[s, b] = tens_part[pl.ds(0, 2 * Q), :]
        send(("oc", s, b), core_send.at[s, b], core_recv.at[s, b], core, 2 * Q, 2)

    def send_z(s, o, ry, rows):
        i = 2 * o + ry
        zsend[s, i] = rows.astype(bf16)
        send(("oz", s), zsend.at[s, i], zrecv.at[s, i], at_z(o, ry), OWN)
        summed[s].append(i)

    def reduce_c(b, s):
        arrived("oc", s, b)
        total = core_own[s, b] + core_recv[s, b]
        if (b, s) in DIRECT_REDUCE:
            for k, o in enumerate(OFFSETS[b]):
                for ry in range(2):
                    i = ry * Q + k * OWN
                    if o or ry:
                        send_z(s, o, ry, total[i : i + OWN])
                    else:
                        fin_own[s] = total[i : i + OWN]
        else:
            ylo_send[s, b] = total[Q:].astype(bf16)
            send(("oy", s, b), ylo_send.at[s, b], ylo_recv.at[s, b], at_z(0, 1), Q)
            core_own[s, b, pl.ds(0, Q), :] = total[:Q]

    def reduce_y(b, s):
        if (b, s) in DIRECT_REDUCE:
            return
        arrived("oy", s, b)
        total = core_own[s, b, pl.ds(0, Q), :] + ylo_recv[s, b].astype(f32)
        for k, o in enumerate(OFFSETS[b]):
            rows = total[k * OWN : (k + 1) * OWN]
            if o:
                send_z(s, o, 0, rows)
            else:
                fin_own[s] = rows

    summed = [[], []]

    def finish(s):
        arrived("oz", s)
        total = fin_own[s]
        for i in sorted(summed[s]):
            total = total + zrecv[s, i].astype(f32)
        (out_ref, ing_ref)[s][...] = total.astype(bf16)

    def weight_grad(m, s):
        left, right = (acts, mids) if s == 0 else (mids, acts)
        rows = pl.ds(m * TM, TM)
        (wing_ref, woutg_ref)[s][rows, :] = lax.dot_general(
            left[0, :, rows], right[1], (((0,), (0,)), ((), ())), preferred_element_type=f32
        ).astype(bf16)

    stages = {
        "sg": start_gather, "gy": gather_y, "gc": gather_c, "p1": first_product,
        "po": pass_on, "rx": reduce_x, "mi": middle, "fy": forward_y, "fr": forward_right,
        "fl": forward_left, "p2": second_product, "rc": reduce_c, "ry": reduce_y,
        "wg": weight_grad, "fi": finish,
    }
    for load in loads[:2]:
        load.wait()
    for name, *args in ORDER:
        stages[name](*args)
    all_left()
    assert (len(landing), len(leaving)) == (N_LAND, N_LEAVE), (len(landing), len(leaving))


def block(tokens, w_in, w_out, cotangent):
    bf16, f32 = jnp.bfloat16, jnp.float32
    hbm = pl.BlockSpec(memory_space=pltpu.HBM)
    vmem = pl.BlockSpec(memory_space=pltpu.VMEM)
    weight = pltpu.VMEM((W, W), bf16)
    own = pltpu.VMEM((OWN, W), bf16)
    return pl.pallas_call(
        block_kernel,
        out_shape=(own, own, weight, weight),
        in_specs=[hbm] * 4,
        out_specs=(vmem,) * 4,
        scratch_shapes=[
            pltpu.VMEM((W, W), bf16),
            pltpu.VMEM((W, W), bf16),
            pltpu.VMEM((2, ROWS, W), bf16),
            pltpu.VMEM((2, NB, RB, W), f32),
            pltpu.VMEM((2, ROWS, W), bf16),
            pltpu.VMEM((2, NB, 6, YR, W), bf16),
            pltpu.VMEM((2, NB, YR, W), bf16),
            pltpu.VMEM((2, NB, YR, W), bf16),
            pltpu.VMEM((2, NB, 2, YR, W), f32),
            pltpu.VMEM((NB, YR, W), f32),
            pltpu.VMEM((2, ROWS, W), bf16),
            pltpu.VMEM((2, NB, 2 * Q, W), f32),
            pltpu.VMEM((2, NB, 2 * Q, W), f32),
            pltpu.VMEM((2, NB, 2 * Q, W), f32),
            pltpu.VMEM((RB, W), f32),
            pltpu.VMEM((2, NB, Q, W), bf16),
            pltpu.VMEM((2, NB, Q, W), bf16),
            pltpu.VMEM((2, OWN, W), f32),
            pltpu.VMEM((2, NZ * 2, OWN, W), bf16),
            pltpu.VMEM((2, NZ * 2, OWN, W), bf16),
            pltpu.SemaphoreType.DMA((4,)),
            pltpu.SemaphoreType.DMA((N_LEAVE,)),
            pltpu.SemaphoreType.DMA((N_LAND,)),
        ],
        compiler_params=pltpu.CompilerParams(
            collective_id=0, has_side_effects=True, vmem_limit_bytes=42 << 20
        ),
        cost_estimate=pl.CostEstimate(
            flops=12 * ROWS * W * W, bytes_accessed=12 << 20, transcendentals=0
        ),
        name="mlp_block",
    )(tokens, w_in, w_out, cotangent)


def store_kernel(*refs):
    n = len(refs) // 2
    sems = refs[-1]
    copies = []
    for source, target in zip(refs[:n], refs[n:-1]):
        for rows in range(0, source.shape[0], STORE_ROWS):
            piece = pl.ds(rows, min(STORE_ROWS, source.shape[0]))
            copies.append(
                pltpu.make_async_copy(source.at[piece], target.at[piece], sems.at[len(copies)])
            )
    for copy in copies:
        copy.start()
    for copy in copies:
        copy.wait()


def store(*arrays):
    hbm = pl.BlockSpec(memory_space=pltpu.HBM)
    return pl.pallas_call(
        store_kernel,
        out_shape=tuple(jax.ShapeDtypeStruct(a.shape, a.dtype) for a in arrays),
        in_specs=[pl.BlockSpec(memory_space=pltpu.VMEM)] * len(arrays),
        out_specs=(hbm,) * len(arrays),
        scratch_shapes=[pltpu.SemaphoreType.DMA((2 + 2 * W // STORE_ROWS,))],
        compiler_params=pltpu.CompilerParams(vmem_limit_bytes=1 << 20),
        name="store",
    )(*arrays)


def on_device(tokens, w_in, w_out, cotangent):
    args = [pltpu.with_memory_space_constraint(a, pltpu.HBM) for a in (tokens, w_in, w_out, cotangent)]
    return store(*block(*args))


def solution(mesh):
    in_specs = (P("tensor", "dp"), P("dp", "tensor"), P("tensor", "dp"), P("tensor", "dp"))
    out_specs = (P("tensor", "dp"), P("tensor", "dp"), P("dp", "tensor"), P("tensor", "dp"))
    return jax.shard_map(
        on_device, mesh=mesh, in_specs=in_specs, out_specs=out_specs, check_vma=False
    )
```
